32 devices in a mesh: tm: 8 (over z, x), chan: 4 (over y, core).
Axes of the slice: x: 2, y: 2, z: 4, core: 2. Of those that a mesh axis runs over, the one named last changes fastest.
Arguments:
- record: bfloat16 [98304, 512], P('tm', 'chan')
- window_starts: int32 [32], P('tm'), may hold values from 0 to 86016, as said below
- alive_mask: int32 [512], P('chan'), may hold values 0 or 1
Outputs:
- stacked: float32 [2, 288, 512, 512], P(None, 'tm', 'chan')
The draws below stay inside these ranges and needn't reach their ends.
Inputs may be any that keep to these rules, and one draw needn't show every extreme that they name: `window_starts`: window k starts at a sample of k // 4 * 12288 to (k // 4 + 1) * 12288 - 1, and every window ends inside the record.
All inputs are finite; a program needn't handle non-finite values. No bound on the sum of `alive_mask` on one device may be relied on, other than what follows from the above.
Results may differ from the reference program's by a relative error of at most 0.0037.
Values may be sent and summed in bfloat16 or wider, within the bound.
A program may use at most 320 MiB of HBM per device.

```python
import math
import jax
import jax.numpy as jnp
from jax import lax

WIN = 12288
KEEP = 288
FLO = 61
HALF = 32
BAND = 512
CH_DEV = 128
WPD = 4
CH = 512
TIME = 98304
WINDOWS = 32


def draw_record(key, part):
    key_noise, key_channel, key_block = jax.random.split(key, 3)
    block_count = TIME // 64
    noise_field = jax.random.normal(key_noise, (block_count, 64, CH), jnp.float32)
    channel_scale = jnp.exp(jax.random.uniform(key_channel, (1, 1, CH), jnp.float32, 0.0, math.log(10.0)))
    mixed = noise_field * channel_scale
    block_scale = jnp.exp(jax.random.uniform(key_block, (block_count, 1, 1), jnp.float32, 0.0, math.log(10.0)))
    return (mixed * block_scale).reshape(TIME, CH).astype(jnp.bfloat16)


def draw_window_starts(key, part):
    offsets = jax.random.randint(key, (WINDOWS,), 0, WIN, jnp.int32)
    group_index = jnp.arange(WINDOWS, dtype=jnp.int32) // WPD
    return jnp.minimum(group_index * WIN + offsets, TIME - WIN).astype(jnp.int32)


def with_ends(drawn, rng, smallest, high):
    longest = drawn.shape.index(max(drawn.shape))
    spots = []
    for shift in (0, 1):
        where = [jax.random.randint(jax.random.fold_in(rng, axis), (), 0, length) for axis, length in enumerate(drawn.shape)]
        where[longest] = (where[longest] + shift) % drawn.shape[longest]
        spots.append(tuple(where))
    return drawn.at[spots[0]].set(smallest).at[spots[1]].set(high)


def setup_inputs(seed: int = 0) -> dict:
    key_of = jax.random.split(jax.random.key(seed), 4)
    record = draw_record(jax.random.fold_in(key_of[3], 71), 0)
    window_starts = draw_window_starts(jax.random.fold_in(key_of[3], 71), 0)
    alive_mask = with_ends((jax.random.randint(key_of[2], (CH,), 0, 10) < 9).astype(jnp.int32), jax.random.fold_in(key_of[2], 1), 0, 1)
    return dict(record=record, window_starts=window_starts, alive_mask=alive_mask)


epsilon = 1e-06

def taper_table(window_length, first_bin, bin_count, first_time, block_length):
    sample_times = first_time + lax.iota(jnp.int32, block_length)
    bin_numbers = first_bin + lax.iota(jnp.int32, bin_count)
    phases = bin_numbers[:, None] * sample_times[None, :] % window_length
    angles = 2.0 * math.pi / window_length * phases.astype(jnp.float32)
    tapering = 0.5 - 0.5 * jnp.cos(2.0 * math.pi / window_length * sample_times.astype(jnp.float32))
    cosine = (tapering[None, :] * jnp.cos(angles)).astype(jnp.bfloat16)
    sine_rows = (-tapering[None, :] * jnp.sin(angles)).astype(jnp.bfloat16)
    return jnp.concatenate([cosine, sine_rows], 0)

def smoother_matrix():
    row_index = lax.iota(jnp.int32, KEEP)[:, None]
    column_index = lax.iota(jnp.int32, KEEP + 2 * HALF)[None, :]
    inside = (column_index >= row_index) & (column_index <= row_index + 2 * HALF)
    return inside.astype(jnp.float32)

def whiten(spectra, alive_mask):
    bin_count = KEEP + 2 * HALF
    real_part = spectra[:, :bin_count]
    imag_part = spectra[:, bin_count:]
    magnitude = jnp.sqrt(real_part * real_part + imag_part * imag_part)
    smoothed = jnp.einsum('kj,wjc->wkc', smoother_matrix(), magnitude, precision=lax.Precision.HIGHEST) / (2 * HALF + 1)
    scaling = alive_mask.astype(jnp.float32)[None, None, :] / (smoothed + epsilon)
    white_real = real_part[:, HALF:HALF + KEEP] * scaling
    white_imag = imag_part[:, HALF:HALF + KEEP] * scaling
    return jnp.stack([white_real, white_imag], 2).astype(jnp.bfloat16)

def diagonals(gram, band_width):
    row_count, span_count = (gram.shape[-2], gram.shape[-1])
    flattened = gram.reshape(gram.shape[:-2] + (row_count * span_count,))
    widths = [(0, 0)] * (flattened.ndim - 1) + [(0, row_count)]
    flattened = jnp.pad(flattened, widths)
    skewed = flattened.reshape(gram.shape[:-2] + (row_count, span_count + 1))
    return skewed[..., :band_width]

def reference(record, window_starts, alive_mask):
    lookup = taper_table(WIN, FLO - HALF, KEEP + 2 * HALF, 0, WIN).astype(jnp.float32)

    def transform_one(window_start):
        frame = lax.dynamic_slice_in_dim(record, window_start.astype(jnp.int32), WIN, 0).astype(jnp.float32)
        return jnp.dot(lookup, frame, preferred_element_type=jnp.float32)
    spectra = lax.map(transform_one, window_starts)
    whitened = whiten(spectra, alive_mask)
    by_frequency = jnp.transpose(whitened, (1, 0, 2, 3))

    def cross_one(frequency_rows):
        values = frequency_rows.astype(jnp.float32)
        rotated = jnp.stack([values[:, 1], -values[:, 0]], 1)
        extended = jnp.pad(values, ((0, 0), (0, 0), (0, BAND)))
        real_blocks = []
        imag_blocks = []
        for block_number in range(CH // CH_DEV):
            first = block_number * CH_DEV
            own_rows = values[:, :, first:first + CH_DEV]
            own_rotated = rotated[:, :, first:first + CH_DEV]
            partner = extended[:, :, first:first + CH_DEV + BAND]
            real_gram = jnp.einsum('wrc,wrj->cj', own_rows, partner)
            imag_gram = jnp.einsum('wrc,wrj->cj', own_rotated, partner)
            real_blocks.append(diagonals(real_gram, BAND))
            imag_blocks.append(diagonals(imag_gram, BAND))
        return jnp.stack([jnp.concatenate(real_blocks, 0), jnp.concatenate(imag_blocks, 0)], 0)
    crossed = lax.map(cross_one, by_frequency)
    return jnp.transpose(crossed, (1, 0, 2, 3)) / WINDOWS
```

```python
import functools
import math

import jax
import jax.numpy as jnp
from jax import lax
from jax.experimental import pallas as pl
from jax.experimental.pallas import tpu as pltpu
from jax.sharding import PartitionSpec as P

KEEP = 288
FLO = 61
HALF = 32
BAND = 512
WPD = 4


epsilon = 1e-06


def passed_along(block, axis, distance):
    devices = range(lax.axis_size(axis))
    route = [(i - distance, i) for i in devices if i - distance in devices]
    return lax.ppermute(block, axis, route)


def build_tables(window_length):
    bin_count = KEEP + 2 * HALF
    block_length = math.gcd(window_length, 2048)
    step_angle = 2.0 * math.pi / window_length
    bin_numbers = FLO - HALF + lax.iota(jnp.int32, bin_count)
    base_times = lax.iota(jnp.int32, block_length)
    base_phases = bin_numbers[:, None] * base_times[None, :] % window_length
    base_angles = step_angle * base_phases.astype(jnp.float32)
    base_cos = jnp.cos(base_angles)
    base_sin = jnp.sin(base_angles)
    tables = []
    for first_time in range(0, window_length, block_length):
        shift_phases = bin_numbers * first_time % window_length
        shift_angles = step_angle * shift_phases.astype(jnp.float32)
        shift_cos = jnp.cos(shift_angles)[:, None]
        shift_sin = jnp.sin(shift_angles)[:, None]
        sample_times = (first_time + base_times).astype(jnp.float32)
        tapering = (0.5 - 0.5 * jnp.cos(step_angle * sample_times))[None, :]
        cos_values = base_cos * shift_cos - base_sin * shift_sin
        sin_values = base_sin * shift_cos + base_cos * shift_sin
        cosine = (tapering * cos_values).astype(jnp.bfloat16)
        sine_rows = (-tapering * sin_values).astype(jnp.bfloat16)
        tables.append(jnp.concatenate([cosine, sine_rows], 0))
    return (tables, block_length)


def smoother_matrix():
    row_index = lax.iota(jnp.int32, KEEP)[:, None]
    column_index = lax.iota(jnp.int32, KEEP + 2 * HALF)[None, :]
    inside = (column_index >= row_index) & (column_index <= row_index + 2 * HALF)
    return inside.astype(jnp.float32)


def whiten(spectra, alive_mask):
    bin_count = KEEP + 2 * HALF
    real_part = spectra[:, :bin_count]
    imag_part = spectra[:, bin_count:]
    magnitude = jnp.sqrt(real_part * real_part + imag_part * imag_part)
    smoothed = jnp.einsum(
        "kj,wjc->wkc", smoother_matrix(), magnitude, precision=lax.Precision.HIGHEST
    ) / (2 * HALF + 1)
    scaling = alive_mask.astype(jnp.float32)[None, None, :] / (smoothed + epsilon)
    white_real = real_part[:, HALF : HALF + KEEP] * scaling
    white_imag = imag_part[:, HALF : HALF + KEEP] * scaling
    whitened = jnp.concatenate([white_real, white_imag], 0).astype(jnp.bfloat16)
    return jnp.transpose(whitened, (1, 0, 2))


def transform(frames, tables, block_length):
    bin_count = KEEP + 2 * HALF
    totals = jnp.zeros((frames.shape[0], 2 * bin_count, frames.shape[2]), jnp.float32)
    for number, lookup in enumerate(tables):
        first_time = number * block_length
        segment = frames[:, first_time : first_time + block_length]
        totals = totals + jnp.einsum(
            "ft,wtc->wfc", lookup, segment, preferred_element_type=jnp.float32
        )
    return totals


def gram_kernel(piece_count, *refs):
    pieces = refs[:piece_count]
    out_ref = refs[piece_count]
    bins, rows, width = pieces[0].shape
    band = out_ref.shape[3]
    window_count = rows // 2
    row = lax.broadcasted_iota(jnp.int32, (rows, rows), 0)
    column = lax.broadcasted_iota(jnp.int32, (rows, rows), 1)
    first_half = row % 8 < 4
    swap = jnp.where(
        first_half & (column == row + 4),
        1.0,
        jnp.where(~first_half & (column == row - 4), -1.0, 0.0),
    ).astype(jnp.bfloat16)
    lane = lax.broadcasted_iota(jnp.int32, (width, width), 0)
    mirror_lane = lax.broadcasted_iota(jnp.int32, (width, width), 1)
    mirror = jnp.where(lane + mirror_lane == width - 1, 1.0, 0.0).astype(jnp.bfloat16)
    upside_down = 7 - lax.broadcasted_iota(jnp.int32, (8, band), 0)
    contract = (((0,), (0,)), ((), ()))
    span = piece_count * width
    for f in range(bins):
        own = jnp.dot(pieces[0][f], mirror, preferred_element_type=jnp.float32).astype(jnp.bfloat16)
        rotated = jnp.dot(swap, own, preferred_element_type=jnp.float32).astype(jnp.bfloat16)
        joined = jnp.concatenate([piece[f] for piece in pieces], 1)
        if span < band + width:
            joined = jnp.concatenate(
                [joined, jnp.zeros((rows, band + width - span), jnp.bfloat16)], 1
            )
        for part, left in enumerate((own, rotated)):
            gram = lax.dot_general(left, joined, contract, preferred_element_type=jnp.float32)
            skewed = pltpu.roll(gram, band + 1, 1, stride=1, stride_axis=0)
            for first in range(0, width, 8):
                rows_of_eight = skewed[width - 8 - first : width - first, :band]
                out_ref[part, f, first : first + 8] = jnp.take_along_axis(
                    rows_of_eight, upside_down, axis=0
                ) * (1.0 / window_count)


def stacked_bands(pieces):
    bins, rows, width = pieces[0].shape
    block = 2
    return pl.pallas_call(
        functools.partial(gram_kernel, len(pieces)),
        grid=(bins // block,),
        in_specs=[pl.BlockSpec((block, rows, width), lambda i: (i, 0, 0))] * len(pieces),
        out_specs=pl.BlockSpec((2, block, width, BAND), lambda i: (0, i, 0, 0)),
        out_shape=jax.ShapeDtypeStruct((2, bins, width, BAND), jnp.float32),
        compiler_params=pltpu.CompilerParams(vmem_limit_bytes=48 * 2**20),
        name="stacked_bands",
    )(*pieces)


def local(record, window_starts, alive_mask):
    window_length = record.shape[0]
    local_width = record.shape[1]
    tables, block_length = build_tables(window_length)
    index_time = lax.axis_index("tm")
    offsets = window_starts - index_time * window_length
    following = passed_along(record, "tm", -1)
    joined = jnp.concatenate([record, following], 0)
    frames = jnp.stack(
        [
            lax.dynamic_slice_in_dim(joined, offsets[number], window_length, 0)
            for number in range(WPD)
        ]
    )
    spectra = transform(frames, tables, block_length)
    whitened = whiten(spectra, alive_mask)
    regrouped = lax.all_to_all(whitened, "tm", split_axis=0, concat_axis=1, tiled=True)
    reach_count = BAND // local_width
    pieces = [regrouped]
    for distance in range(1, min(reach_count + 1, lax.axis_size("chan"))):
        pieces.append(passed_along(regrouped, "chan", -distance))
    return stacked_bands(pieces)


def solution(mesh):
    return jax.shard_map(
        local,
        mesh=mesh,
        in_specs=(P("tm", "chan"), P("tm"), P("chan")),
        out_specs=P(None, "tm", "chan", None),
        check_vma=False,
    )
```

```python
import functools
import math

import jax
import jax.numpy as jnp
import numpy as np
from jax import lax
from jax.experimental import pallas as pl
from jax.experimental.pallas import tpu as pltpu
from jax.sharding import PartitionSpec as P

KEEP = 288
FLO = 61
HALF = 32
BAND = 512
WPD = 4


epsilon = 1e-06


def passed_along(block, axis, distance):
    devices = range(lax.axis_size(axis))
    route = [(i - distance, i) for i in devices if i - distance in devices]
    return lax.ppermute(block, axis, route)


def base_tables(window_length, block_length):
    step_angle = 2.0 * np.pi / window_length
    bin_numbers = FLO - HALF + np.arange(KEEP + 2 * HALF)
    times = np.arange(block_length)
    firsts = np.arange(0, window_length, block_length)
    base = step_angle * (bin_numbers[:, None] * times[None, :] % window_length)
    shift = step_angle * (bin_numbers[None, :, None] * firsts[:, None, None] % window_length)
    tapering = 0.5 - 0.5 * np.cos(step_angle * (firsts[:, None, None] + times[None, None, :]))
    values = (np.cos(base), np.sin(base), np.cos(shift), np.sin(shift), tapering)
    return [value.astype(np.float32) for value in values]


def dft_kernel(cos_ref, sin_ref, shift_cos_ref, shift_sin_ref, taper_ref, frames_ref, out_ref):
    bin_count, block_length = cos_ref.shape
    shift_cos = shift_cos_ref[0]
    shift_sin = shift_sin_ref[0]

    @pl.when(pl.program_id(0) == 0)
    def _():
        out_ref[...] = jnp.zeros_like(out_ref)

    pieces = []
    for first in range(0, block_length, 256):
        span = slice(first, first + 256)
        base_cos = cos_ref[:, span]
        base_sin = sin_ref[:, span]
        tapering = taper_ref[0, :, span]
        cosine = tapering * (base_cos * shift_cos - base_sin * shift_sin)
        sine = -tapering * (base_sin * shift_cos + base_cos * shift_sin)
        pieces.append(jnp.concatenate([cosine, sine], 0).astype(jnp.bfloat16))
    lookup = jnp.concatenate(pieces, 1)
    width = frames_ref.shape[2]
    for number in range(0, WPD, 2):
        pair = jnp.concatenate([frames_ref[number], frames_ref[number + 1]], 1)
        out_ref[:, number * width : (number + 2) * width] += jnp.dot(
            lookup, pair, preferred_element_type=jnp.float32
        )


def transform(frames):
    count, window_length, width = frames.shape
    block_length = math.gcd(window_length, 1024)
    bin_count = KEEP + 2 * HALF
    steps = window_length // block_length
    return pl.pallas_call(
        dft_kernel,
        grid=(steps,),
        in_specs=[
            pl.BlockSpec((bin_count, block_length), lambda i: (0, 0)),
            pl.BlockSpec((bin_count, block_length), lambda i: (0, 0)),
            pl.BlockSpec((1, bin_count, 1), lambda i: (i, 0, 0)),
            pl.BlockSpec((1, bin_count, 1), lambda i: (i, 0, 0)),
            pl.BlockSpec((1, 1, block_length), lambda i: (i, 0, 0)),
            pl.BlockSpec((count, block_length, width), lambda i: (0, i, 0)),
        ],
        out_specs=pl.BlockSpec((2 * bin_count, count * width), lambda i: (0, 0)),
        out_shape=jax.ShapeDtypeStruct((2 * bin_count, count * width), jnp.float32),
        compiler_params=pltpu.CompilerParams(vmem_limit_bytes=40 * 2**20),
        cost_estimate=pl.CostEstimate(
            flops=4 * bin_count * count * width * window_length,
            bytes_accessed=2 * count * width * window_length,
            transcendentals=0,
        ),
        name="windowed_transform",
    )(*base_tables(window_length, block_length), frames)


def smoother_matrix():
    row_index = lax.iota(jnp.int32, KEEP)[:, None]
    column_index = lax.iota(jnp.int32, KEEP + 2 * HALF)[None, :]
    inside = (column_index >= row_index) & (column_index <= row_index + 2 * HALF)
    return inside.astype(jnp.float32)


def whiten(spectra, alive_mask):
    bin_count = KEEP + 2 * HALF
    width = alive_mask.shape[0]
    real_part = spectra[:bin_count]
    imag_part = spectra[bin_count:]
    magnitude = jnp.sqrt(real_part * real_part + imag_part * imag_part)
    smoothed = jnp.dot(smoother_matrix(), magnitude, precision=lax.Precision.HIGHEST)
    smoothed = smoothed / (2 * HALF + 1)
    scaling = jnp.tile(alive_mask.astype(jnp.float32), WPD)[None, :] / (smoothed + epsilon)
    white_real = real_part[HALF : HALF + KEEP] * scaling
    white_imag = imag_part[HALF : HALF + KEEP] * scaling
    whitened = jnp.concatenate([white_real, white_imag], 1).astype(jnp.bfloat16)
    return whitened.reshape(KEEP, 2 * WPD, width)


def gram_kernel(piece_count, *refs):
    pieces = refs[:piece_count]
    out_ref = refs[piece_count]
    bins, rows, width = pieces[0].shape
    band = out_ref.shape[3]
    window_count = rows // 2
    row = lax.broadcasted_iota(jnp.int32, (rows, rows), 0)
    column = lax.broadcasted_iota(jnp.int32, (rows, rows), 1)
    first_half = row % 8 < 4
    swap = jnp.where(
        first_half & (column == row + 4),
        1.0,
        jnp.where(~first_half & (column == row - 4), -1.0, 0.0),
    ).astype(jnp.bfloat16)
    lane = lax.broadcasted_iota(jnp.int32, (width, width), 0)
    mirror_lane = lax.broadcasted_iota(jnp.int32, (width, width), 1)
    mirror = jnp.where(lane + mirror_lane == width - 1, 1.0, 0.0).astype(jnp.bfloat16)
    upside_down = 7 - lax.broadcasted_iota(jnp.int32, (8, band), 0)
    contract = (((0,), (0,)), ((), ()))
    span = piece_count * width
    for f in range(bins):
        own = jnp.dot(pieces[0][f], mirror, preferred_element_type=jnp.float32).astype(jnp.bfloat16)
        rotated = jnp.dot(swap, own, preferred_element_type=jnp.float32).astype(jnp.bfloat16)
        joined = jnp.concatenate([piece[f] for piece in pieces], 1)
        if span < band + width:
            joined = jnp.concatenate(
                [joined, jnp.zeros((rows, band + width - span), jnp.bfloat16)], 1
            )
        for part, left in enumerate((own, rotated)):
            gram = lax.dot_general(left, joined, contract, preferred_element_type=jnp.float32)
            skewed = pltpu.roll(gram, band + 1, 1, stride=1, stride_axis=0)
            for first in range(0, width, 8):
                rows_of_eight = skewed[width - 8 - first : width - first, :band]
                out_ref[part, f, first : first + 8] = jnp.take_along_axis(
                    rows_of_eight, upside_down, axis=0
                ) * (1.0 / window_count)


def stacked_bands(pieces):
    bins, rows, width = pieces[0].shape
    block = 2
    return pl.pallas_call(
        functools.partial(gram_kernel, len(pieces)),
        grid=(bins // block,),
        in_specs=[pl.BlockSpec((block, rows, width), lambda i: (i, 0, 0))] * len(pieces),
        out_specs=pl.BlockSpec((2, block, width, BAND), lambda i: (0, i, 0, 0)),
        out_shape=jax.ShapeDtypeStruct((2, bins, width, BAND), jnp.float32),
        compiler_params=pltpu.CompilerParams(vmem_limit_bytes=48 * 2**20),
        name="stacked_bands",
    )(*pieces)


def cut(joined, offsets, window_length):
    return jnp.stack(
        [
            lax.dynamic_slice_in_dim(joined, offsets[number], window_length, 0)
            for number in range(WPD)
        ]
    )


def local(record, window_starts, alive_mask):
    window_length = record.shape[0]
    local_width = record.shape[1]
    index_time = lax.axis_index("tm")
    offsets = window_starts - index_time * window_length
    earlier_offsets = passed_along(offsets, "tm", 1)
    silence = jnp.zeros_like(record)
    tails = cut(jnp.concatenate([silence, record], 0), earlier_offsets, window_length)
    tail_spectra = transform(tails)
    following = passed_along(tail_spectra, "tm", -1)
    heads = cut(jnp.concatenate([record, silence], 0), offsets, window_length)
    spectra = transform(heads) + following
    whitened = whiten(spectra, alive_mask)
    regrouped = lax.all_to_all(whitened, "tm", split_axis=0, concat_axis=1, tiled=True)
    reach_count = BAND // local_width
    pieces = [regrouped]
    for distance in range(1, min(reach_count + 1, lax.axis_size("chan"))):
        pieces.append(passed_along(regrouped, "chan", -distance))
    return stacked_bands(pieces)


def solution(mesh):
    return jax.shard_map(
        local,
        mesh=mesh,
        in_specs=(P("tm", "chan"), P("tm"), P("chan")),
        out_specs=P(None, "tm", "chan", None),
        check_vma=False,
    )
```

```python
import functools
import math

import jax
import jax.numpy as jnp
import numpy as np
from jax import lax
from jax.experimental import pallas as pl
from jax.experimental.pallas import tpu as pltpu
from jax.sharding import PartitionSpec as P

KEEP = 288
FLO = 61
HALF = 32
BAND = 512
WPD = 4


epsilon = 1e-06


def passed_along(block, axis, distance):
    devices = range(lax.axis_size(axis))
    route = [(i - distance, i) for i in devices if i - distance in devices]
    return lax.ppermute(block, axis, route)


def base_tables(window_length, block_length):
    step_angle = 2.0 * np.pi / window_length
    bin_numbers = FLO - HALF + np.arange(KEEP + 2 * HALF)
    times = np.arange(block_length)
    firsts = np.arange(0, window_length, block_length)
    base = step_angle * (bin_numbers[:, None] * times[None, :] % window_length)
    shift = step_angle * (bin_numbers[None, :, None] * firsts[:, None, None] % window_length)
    tapering = 0.5 - 0.5 * np.cos(step_angle * (firsts[:, None, None] + times[None, None, :]))
    values = (np.cos(base), np.sin(base), np.cos(shift), np.sin(shift), tapering)
    return [value.astype(np.float32) for value in values]


def dft_kernel(tail, windows, offsets_ref, *refs):
    cos_ref, sin_ref, shift_cos_ref, shift_sin_ref, taper_ref, record_ref, out_ref, padded = refs
    bin_count, block_length = cos_ref.shape
    window_length, width = record_ref.shape
    step = pl.program_id(0)
    shift_cos = shift_cos_ref[0]
    shift_sin = shift_sin_ref[0]

    @pl.when(step == 0)
    def _():
        out_ref[...] = jnp.zeros_like(out_ref)

        @pl.loop(0, window_length // block_length)
        def _(number):
            rows = pl.ds(pl.multiple_of(number * block_length, block_length), block_length)
            loud = pl.ds(
                pl.multiple_of(number * block_length + tail * window_length, block_length),
                block_length,
            )
            silent = pl.ds(
                pl.multiple_of(number * block_length + (1 - tail) * window_length, block_length),
                block_length,
            )
            padded[loud, :] = record_ref[rows, :].astype(jnp.float32)
            padded[silent, :] = jnp.zeros((block_length, width), jnp.float32)

    pieces = []
    for first in range(0, block_length, 256):
        span = slice(first, first + 256)
        base_cos = cos_ref[:, span]
        base_sin = sin_ref[:, span]
        tapering = taper_ref[0, :, span]
        cosine = tapering * (base_cos * shift_cos - base_sin * shift_sin)
        sine = -tapering * (base_sin * shift_cos + base_cos * shift_sin)
        pieces.append(jnp.concatenate([cosine, sine], 0).astype(jnp.bfloat16))
    lookup = jnp.concatenate(pieces, 1)
    for number in range(0, len(windows), 2):
        frames = []
        for window in windows[number : number + 2]:
            start = jnp.clip(offsets_ref[window], 0, window_length - 1)
            rows = pl.ds(start + step * block_length, block_length)
            frames.append(padded[rows, :].astype(jnp.bfloat16))
        out_ref[:, number * width : (number + 2) * width] += jnp.dot(
            lookup, jnp.concatenate(frames, 1), preferred_element_type=jnp.float32
        )


def transform(record, offsets, tail, windows):
    window_length, width = record.shape
    count = len(windows)
    block_length = math.gcd(window_length, 1024)
    bin_count = KEEP + 2 * HALF
    steps = window_length // block_length
    return pl.pallas_call(
        functools.partial(dft_kernel, tail, windows),
        grid=(steps,),
        in_specs=[
            pl.BlockSpec(memory_space=pltpu.SMEM),
            pl.BlockSpec((bin_count, block_length), lambda i: (0, 0)),
            pl.BlockSpec((bin_count, block_length), lambda i: (0, 0)),
            pl.BlockSpec((1, bin_count, 1), lambda i: (i, 0, 0)),
            pl.BlockSpec((1, bin_count, 1), lambda i: (i, 0, 0)),
            pl.BlockSpec((1, 1, block_length), lambda i: (i, 0, 0)),
            pl.BlockSpec((window_length, width), lambda i: (0, 0)),
        ],
        out_specs=pl.BlockSpec((2 * bin_count, count * width), lambda i: (0, 0)),
        out_shape=jax.ShapeDtypeStruct((2 * bin_count, count * width), jnp.float32),
        scratch_shapes=[pltpu.VMEM((2 * window_length, width), jnp.float32)],
        compiler_params=pltpu.CompilerParams(vmem_limit_bytes=44 * 2**20),
        cost_estimate=pl.CostEstimate(
            flops=4 * bin_count * count * width * window_length,
            bytes_accessed=2 * width * window_length,
            transcendentals=0,
        ),
        name="windowed_transform",
    )(offsets, *base_tables(window_length, block_length), record)


def smoother_matrix():
    row_index = lax.iota(jnp.int32, KEEP)[:, None]
    column_index = lax.iota(jnp.int32, KEEP + 2 * HALF)[None, :]
    inside = (column_index >= row_index) & (column_index <= row_index + 2 * HALF)
    return inside.astype(jnp.float32)


def whiten(spectra, alive_mask):
    bin_count = KEEP + 2 * HALF
    width = alive_mask.shape[0]
    real_part = spectra[:bin_count]
    imag_part = spectra[bin_count:]
    magnitude = jnp.sqrt(real_part * real_part + imag_part * imag_part)
    smoothed = jnp.dot(smoother_matrix(), magnitude, precision=lax.Precision.HIGHEST)
    smoothed = smoothed / (2 * HALF + 1)
    scaling = jnp.tile(alive_mask.astype(jnp.float32), WPD)[None, :] / (smoothed + epsilon)
    white_real = real_part[HALF : HALF + KEEP] * scaling
    white_imag = imag_part[HALF : HALF + KEEP] * scaling
    whitened = jnp.concatenate([white_real, white_imag], 1).astype(jnp.bfloat16)
    return whitened.reshape(KEEP, 2 * WPD, width)


def gram_kernel(piece_count, *refs):
    pieces = refs[:piece_count]
    out_ref = refs[piece_count]
    bins, rows, width = pieces[0].shape
    band = out_ref.shape[3]
    window_count = rows // 2
    row = lax.broadcasted_iota(jnp.int32, (rows, rows), 0)
    column = lax.broadcasted_iota(jnp.int32, (rows, rows), 1)
    first_half = row % 8 < 4
    swap = jnp.where(
        first_half & (column == row + 4),
        1.0,
        jnp.where(~first_half & (column == row - 4), -1.0, 0.0),
    ).astype(jnp.bfloat16)
    lane = lax.broadcasted_iota(jnp.int32, (width, width), 0)
    mirror_lane = lax.broadcasted_iota(jnp.int32, (width, width), 1)
    mirror = jnp.where(lane + mirror_lane == width - 1, 1.0, 0.0).astype(jnp.bfloat16)
    upside_down = 7 - lax.broadcasted_iota(jnp.int32, (8, band), 0)
    contract = (((0,), (0,)), ((), ()))
    span = piece_count * width
    for f in range(bins):
        own = jnp.dot(pieces[0][f], mirror, preferred_element_type=jnp.float32).astype(jnp.bfloat16)
        rotated = jnp.dot(swap, own, preferred_element_type=jnp.float32).astype(jnp.bfloat16)
        joined = jnp.concatenate([piece[f] for piece in pieces], 1)
        if span < band + width:
            joined = jnp.concatenate(
                [joined, jnp.zeros((rows, band + width - span), jnp.bfloat16)], 1
            )
        for part, left in enumerate((own, rotated)):
            gram = lax.dot_general(left, joined, contract, preferred_element_type=jnp.float32)
            skewed = pltpu.roll(gram, band + 1, 1, stride=1, stride_axis=0)
            for first in range(0, width, 8):
                rows_of_eight = skewed[width - 8 - first : width - first, :band]
                out_ref[part, f, first : first + 8] = jnp.take_along_axis(
                    rows_of_eight, upside_down, axis=0
                ) * (1.0 / window_count)


def stacked_bands(pieces):
    bins, rows, width = pieces[0].shape
    block = 2
    return pl.pallas_call(
        functools.partial(gram_kernel, len(pieces)),
        grid=(bins // block,),
        in_specs=[pl.BlockSpec((block, rows, width), lambda i: (i, 0, 0))] * len(pieces),
        out_specs=pl.BlockSpec((2, block, width, BAND), lambda i: (0, i, 0, 0)),
        out_shape=jax.ShapeDtypeStruct((2, bins, width, BAND), jnp.float32),
        compiler_params=pltpu.CompilerParams(vmem_limit_bytes=48 * 2**20),
        name="stacked_bands",
    )(*pieces)


def local(record, window_starts, alive_mask):
    window_length = record.shape[0]
    local_width = record.shape[1]
    index_time = lax.axis_index("tm")
    offsets = window_starts - index_time * window_length
    earlier_offsets = passed_along(offsets, "tm", 1)
    all_windows = tuple(range(WPD))
    heads = transform(record, offsets, 0, all_windows)
    heads, earlier_offsets = lax.optimization_barrier((heads, earlier_offsets))
    arrived = []
    for windows in (all_windows[: WPD // 2], all_windows[WPD // 2 :]):
        tails = transform(record, earlier_offsets, 1, windows)
        arrived.append(passed_along(tails, "tm", -1))
    spectra = heads + jnp.concatenate(arrived, 1)
    whitened = whiten(spectra, alive_mask)
    regrouped = lax.all_to_all(whitened, "tm", split_axis=0, concat_axis=1, tiled=True)
    reach_count = BAND // local_width
    pieces = [regrouped]
    for distance in range(1, min(reach_count + 1, lax.axis_size("chan"))):
        pieces.append(passed_along(regrouped, "chan", -distance))
    return stacked_bands(pieces)


def solution(mesh):
    return jax.shard_map(
        local,
        mesh=mesh,
        in_specs=(P("tm", "chan"), P("tm"), P("chan")),
        out_specs=P(None, "tm", "chan", None),
        check_vma=False,
    )
```

```python
import functools
import math

import jax
import jax.numpy as jnp
import numpy as np
from jax import lax
from jax.experimental import pallas as pl
from jax.experimental.pallas import tpu as pltpu
from jax.sharding import PartitionSpec as P

KEEP = 288
FLO = 61
HALF = 32
BAND = 512
WPD = 4


epsilon = 1e-06


def passed_along(block, axis, distance):
    devices = range(lax.axis_size(axis))
    route = [(i - distance, i) for i in devices if i - distance in devices]
    return lax.ppermute(block, axis, route)


def base_tables(window_length, block_length):
    step_angle = 2.0 * np.pi / window_length
    bin_numbers = FLO - HALF + np.arange(KEEP + 2 * HALF)
    times = np.arange(block_length)
    firsts = np.arange(0, window_length, block_length)
    base = step_angle * (bin_numbers[:, None] * times[None, :] % window_length)
    shift = step_angle * (bin_numbers[None, :, None] * firsts[:, None, None] % window_length)
    tapering = 0.5 - 0.5 * np.cos(step_angle * (firsts[:, None, None] + times[None, None, :]))
    values = (np.cos(base), np.sin(base), np.cos(shift), np.sin(shift), tapering)
    return [value.astype(np.float32) for value in values]


def dft_kernel(tail, windows, offsets_ref, *refs):
    cos_ref, sin_ref, shift_cos_ref, shift_sin_ref, taper_ref, record_ref, out_ref, padded = refs
    bin_count, block_length = cos_ref.shape
    window_length, width = record_ref.shape
    step = pl.program_id(0)
    shift_cos = shift_cos_ref[0]
    shift_sin = shift_sin_ref[0]

    @pl.when(step == 0)
    def _():
        out_ref[...] = jnp.zeros_like(out_ref)

        @pl.loop(0, window_length // block_length)
        def _(number):
            rows = pl.ds(pl.multiple_of(number * block_length, block_length), block_length)
            loud = pl.ds(
                pl.multiple_of(number * block_length + tail * window_length, block_length),
                block_length,
            )
            silent = pl.ds(
                pl.multiple_of(number * block_length + (1 - tail) * window_length, block_length),
                block_length,
            )
            padded[loud, :] = record_ref[rows, :].astype(jnp.float32)
            padded[silent, :] = jnp.zeros((block_length, width), jnp.float32)

    pieces = []
    for first in range(0, block_length, 256):
        span = slice(first, first + 256)
        base_cos = cos_ref[:, span]
        base_sin = sin_ref[:, span]
        tapering = taper_ref[0, :, span]
        cosine = tapering * (base_cos * shift_cos - base_sin * shift_sin)
        sine = -tapering * (base_sin * shift_cos + base_cos * shift_sin)
        pieces.append(jnp.concatenate([cosine, sine], 0).astype(jnp.bfloat16))
    lookup = jnp.concatenate(pieces, 1)
    for number in range(0, len(windows), 2):
        frames = []
        for window in windows[number : number + 2]:
            start = jnp.clip(offsets_ref[window], 0, window_length - 1)
            rows = pl.ds(start + step * block_length, block_length)
            frames.append(padded[rows, :].astype(jnp.bfloat16))
        out_ref[:, number * width : (number + 2) * width] += jnp.dot(
            lookup, jnp.concatenate(frames, 1), preferred_element_type=jnp.float32
        )


def transform(record, offsets, tail, windows):
    window_length, width = record.shape
    count = len(windows)
    block_length = math.gcd(window_length, 1024)
    bin_count = KEEP + 2 * HALF
    steps = window_length // block_length
    return pl.pallas_call(
        functools.partial(dft_kernel, tail, windows),
        grid=(steps,),
        in_specs=[
            pl.BlockSpec(memory_space=pltpu.SMEM),
            pl.BlockSpec((bin_count, block_length), lambda i: (0, 0)),
            pl.BlockSpec((bin_count, block_length), lambda i: (0, 0)),
            pl.BlockSpec((1, bin_count, 1), lambda i: (i, 0, 0)),
            pl.BlockSpec((1, bin_count, 1), lambda i: (i, 0, 0)),
            pl.BlockSpec((1, 1, block_length), lambda i: (i, 0, 0)),
            pl.BlockSpec((window_length, width), lambda i: (0, 0)),
        ],
        out_specs=pl.BlockSpec((2 * bin_count, count * width), lambda i: (0, 0)),
        out_shape=jax.ShapeDtypeStruct((2 * bin_count, count * width), jnp.float32),
        scratch_shapes=[pltpu.VMEM((2 * window_length, width), jnp.float32)],
        compiler_params=pltpu.CompilerParams(vmem_limit_bytes=44 * 2**20),
        cost_estimate=pl.CostEstimate(
            flops=4 * bin_count * count * width * window_length,
            bytes_accessed=2 * width * window_length,
            transcendentals=0,
        ),
        name="windowed_transform",
    )(offsets, *base_tables(window_length, block_length), record)


def smoother_matrix():
    row_index = lax.iota(jnp.int32, KEEP)[:, None]
    column_index = lax.iota(jnp.int32, KEEP + 2 * HALF)[None, :]
    inside = (column_index >= row_index) & (column_index <= row_index + 2 * HALF)
    return inside.astype(jnp.float32)


def whiten(spectra, alive_mask):
    bin_count = KEEP + 2 * HALF
    width = alive_mask.shape[0]
    real_part = spectra[:bin_count]
    imag_part = spectra[bin_count:]
    magnitude = jnp.sqrt(real_part * real_part + imag_part * imag_part)
    smoothed = jnp.dot(smoother_matrix(), magnitude, precision=lax.Precision.HIGHEST)
    smoothed = smoothed / (2 * HALF + 1)
    scaling = jnp.tile(alive_mask.astype(jnp.float32), WPD)[None, :] / (smoothed + epsilon)
    white_real = real_part[HALF : HALF + KEEP] * scaling
    white_imag = imag_part[HALF : HALF + KEEP] * scaling
    whitened = jnp.concatenate([white_real, white_imag], 1).astype(jnp.bfloat16)
    return whitened.reshape(KEEP, 2 * WPD, width)


def gram_kernel(piece_count, *refs):
    pieces = refs[:piece_count]
    out_ref = refs[piece_count]
    bins, rows, width = pieces[0].shape
    band = out_ref.shape[3]
    window_count = rows // 2
    row = lax.broadcasted_iota(jnp.int32, (rows, rows), 0)
    column = lax.broadcasted_iota(jnp.int32, (rows, rows), 1)
    first_half = row % 8 < 4
    swap = jnp.where(
        first_half & (column == row + 4),
        1.0,
        jnp.where(~first_half & (column == row - 4), -1.0, 0.0),
    ).astype(jnp.bfloat16)
    lane = lax.broadcasted_iota(jnp.int32, (width, width), 0)
    mirror_lane = lax.broadcasted_iota(jnp.int32, (width, width), 1)
    mirror = jnp.where(lane + mirror_lane == width - 1, 1.0, 0.0).astype(jnp.bfloat16)
    upside_down = 7 - lax.broadcasted_iota(jnp.int32, (8, band), 0)
    contract = (((0,), (0,)), ((), ()))
    span = piece_count * width
    for f in range(bins):
        own = jnp.dot(pieces[0][f], mirror, preferred_element_type=jnp.float32).astype(jnp.bfloat16)
        rotated = jnp.dot(swap, own, preferred_element_type=jnp.float32).astype(jnp.bfloat16)
        joined = jnp.concatenate([piece[f] for piece in pieces], 1)
        if span < band + width:
            joined = jnp.concatenate(
                [joined, jnp.zeros((rows, band + width - span), jnp.bfloat16)], 1
            )
        for part, left in enumerate((own, rotated)):
            gram = lax.dot_general(left, joined, contract, preferred_element_type=jnp.float32)
            skewed = pltpu.roll(gram, band + 1, 1, stride=1, stride_axis=0)
            for first in range(0, width, 8):
                rows_of_eight = skewed[width - 8 - first : width - first, :band]
                out_ref[part, f, first : first + 8] = jnp.take_along_axis(
                    rows_of_eight, upside_down, axis=0
                ) * (1.0 / window_count)


def stacked_bands(pieces):
    bins, rows, width = pieces[0].shape
    block = 2
    return pl.pallas_call(
        functools.partial(gram_kernel, len(pieces)),
        grid=(bins // block,),
        in_specs=[pl.BlockSpec((block, rows, width), lambda i: (i, 0, 0))] * len(pieces),
        out_specs=pl.BlockSpec((2, block, width, BAND), lambda i: (0, i, 0, 0)),
        out_shape=jax.ShapeDtypeStruct((2, bins, width, BAND), jnp.float32),
        compiler_params=pltpu.CompilerParams(vmem_limit_bytes=48 * 2**20),
        name="stacked_bands",
    )(*pieces)


def local(record, window_starts, alive_mask):
    window_length = record.shape[0]
    local_width = record.shape[1]
    index_time = lax.axis_index("tm")
    offsets = window_starts - index_time * window_length
    earlier_offsets = passed_along(offsets, "tm", 1)
    all_windows = tuple(range(WPD))
    tails = transform(record, earlier_offsets, 1, all_windows)
    following = passed_along(tails, "tm", -1)
    spectra = transform(record, offsets, 0, all_windows) + following
    whitened = whiten(spectra, alive_mask)
    regrouped = lax.all_to_all(whitened, "tm", split_axis=0, concat_axis=1, tiled=True)
    reach_count = BAND // local_width
    pieces = [regrouped]
    for distance in range(1, min(reach_count + 1, lax.axis_size("chan"))):
        pieces.append(passed_along(regrouped, "chan", -distance))
    return stacked_bands(pieces)


def solution(mesh):
    return jax.shard_map(
        local,
        mesh=mesh,
        in_specs=(P("tm", "chan"), P("tm"), P("chan")),
        out_specs=P(None, "tm", "chan", None),
        check_vma=False,
    )
```

```python
import functools
import math

import jax
import jax.numpy as jnp
import numpy as np
from jax import lax
from jax.experimental import pallas as pl
from jax.experimental.pallas import tpu as pltpu
from jax.sharding import PartitionSpec as P

KEEP = 288
FLO = 61
HALF = 32
BAND = 512
WPD = 4


epsilon = 1e-06


def passed_along(block, axis, distance):
    devices = range(lax.axis_size(axis))
    route = [(i - distance, i) for i in devices if i - distance in devices]
    return lax.ppermute(block, axis, route)


def base_tables(window_length, block_length):
    step_angle = 2.0 * np.pi / window_length
    bin_numbers = FLO - HALF + np.arange(KEEP + 2 * HALF)
    times = np.arange(block_length)
    firsts = np.arange(0, window_length, block_length)
    base = step_angle * (bin_numbers[:, None] * times[None, :] % window_length)
    shift = step_angle * (bin_numbers[None, :, None] * firsts[:, None, None] % window_length)
    tapering = 0.5 - 0.5 * np.cos(step_angle * (firsts[:, None, None] + times[None, None, :]))
    values = (np.cos(base), np.sin(base), np.cos(shift), np.sin(shift), tapering)
    return [value.astype(np.float32) for value in values]


def dft_kernel(tail, windows, offsets_ref, *refs):
    cos_ref, sin_ref, shift_cos_ref, shift_sin_ref, taper_ref, record_ref, out_ref, padded = refs
    bin_count, block_length = cos_ref.shape
    window_length, width = record_ref.shape
    step = pl.program_id(0)
    shift_cos = shift_cos_ref[0]
    shift_sin = shift_sin_ref[0]

    @pl.when(step == 0)
    def _():
        out_ref[...] = jnp.zeros_like(out_ref)

        @pl.loop(0, window_length // block_length)
        def _(number):
            rows = pl.ds(pl.multiple_of(number * block_length, block_length), block_length)
            loud = pl.ds(
                pl.multiple_of(number * block_length + tail * window_length, block_length),
                block_length,
            )
            silent = pl.ds(
                pl.multiple_of(number * block_length + (1 - tail) * window_length, block_length),
                block_length,
            )
            padded[loud, :] = record_ref[rows, :].astype(jnp.float32)
            padded[silent, :] = jnp.zeros((block_length, width), jnp.float32)

    pieces = []
    for first in range(0, block_length, 256):
        span = slice(first, first + 256)
        base_cos = cos_ref[:, span]
        base_sin = sin_ref[:, span]
        tapering = taper_ref[0, :, span]
        cosine = tapering * (base_cos * shift_cos - base_sin * shift_sin)
        sine = -tapering * (base_sin * shift_cos + base_cos * shift_sin)
        pieces.append(jnp.concatenate([cosine, sine], 0).astype(jnp.bfloat16))
    lookup = jnp.concatenate(pieces, 1)
    for number in range(0, len(windows), 2):
        frames = []
        for window in windows[number : number + 2]:
            start = jnp.clip(offsets_ref[window], 0, window_length - 1)
            rows = pl.ds(start + step * block_length, block_length)
            frames.append(padded[rows, :].astype(jnp.bfloat16))
        out_ref[:, number * width : (number + 2) * width] += jnp.dot(
            lookup, jnp.concatenate(frames, 1), preferred_element_type=jnp.float32
        )


def transform(record, offsets, tail, windows):
    window_length, width = record.shape
    count = len(windows)
    block_length = math.gcd(window_length, 1024)
    bin_count = KEEP + 2 * HALF
    steps = window_length // block_length
    return pl.pallas_call(
        functools.partial(dft_kernel, tail, windows),
        grid=(steps,),
        in_specs=[
            pl.BlockSpec(memory_space=pltpu.SMEM),
            pl.BlockSpec((bin_count, block_length), lambda i: (0, 0)),
            pl.BlockSpec((bin_count, block_length), lambda i: (0, 0)),
            pl.BlockSpec((1, bin_count, 1), lambda i: (i, 0, 0)),
            pl.BlockSpec((1, bin_count, 1), lambda i: (i, 0, 0)),
            pl.BlockSpec((1, 1, block_length), lambda i: (i, 0, 0)),
            pl.BlockSpec((window_length, width), lambda i: (0, 0)),
        ],
        out_specs=pl.BlockSpec((2 * bin_count, count * width), lambda i: (0, 0)),
        out_shape=jax.ShapeDtypeStruct((2 * bin_count, count * width), jnp.float32),
        scratch_shapes=[pltpu.VMEM((2 * window_length, width), jnp.float32)],
        compiler_params=pltpu.CompilerParams(vmem_limit_bytes=44 * 2**20),
        cost_estimate=pl.CostEstimate(
            flops=4 * bin_count * count * width * window_length,
            bytes_accessed=2 * width * window_length,
            transcendentals=0,
        ),
        name="windowed_transform",
    )(offsets, *base_tables(window_length, block_length), record)


def smoother_matrix():
    row_index = lax.iota(jnp.int32, KEEP)[:, None]
    column_index = lax.iota(jnp.int32, KEEP + 2 * HALF)[None, :]
    inside = (column_index >= row_index) & (column_index <= row_index + 2 * HALF)
    return inside.astype(jnp.float32)


def whiten(spectra, alive_mask):
    bin_count = KEEP + 2 * HALF
    width = alive_mask.shape[0]
    real_part = spectra[:bin_count]
    imag_part = spectra[bin_count:]
    magnitude = jnp.sqrt(real_part * real_part + imag_part * imag_part)
    smoothed = jnp.dot(smoother_matrix(), magnitude, precision=lax.Precision.HIGHEST)
    smoothed = smoothed / (2 * HALF + 1)
    scaling = jnp.tile(alive_mask.astype(jnp.float32), WPD)[None, :] / (smoothed + epsilon)
    white_real = real_part[HALF : HALF + KEEP] * scaling
    white_imag = imag_part[HALF : HALF + KEEP] * scaling
    whitened = jnp.concatenate([white_real, white_imag], 1).astype(jnp.bfloat16)
    return whitened.reshape(KEEP, 2 * WPD, width)


def gather_kernel(time_count, chan_count, white_ref, out_ref, sends, arrivals, hops, landings):
    piece_count = out_ref.shape[0]
    me_time = lax.axis_index("tm")
    me_chan = lax.axis_index("chan")
    below = lax.rem(me_chan + chan_count - 1, chan_count)
    above = lax.rem(me_chan + 1, chan_count)

    def signal(time, chan):
        pl.semaphore_signal(
            barrier, inc=1, device_id=(time, chan), device_id_type=pl.DeviceIdType.MESH
        )

    barrier = pltpu.get_barrier_semaphore()
    for distance in range(1, time_count):
        signal(lax.rem(me_time + distance, time_count), me_chan)
    signal(me_time, below)
    signal(me_time, above)
    pl.semaphore_wait(barrier, time_count + 1)

    def regroup(distance):
        target = lax.rem(me_time + distance, time_count)
        return pltpu.make_async_remote_copy(
            src_ref=white_ref.at[target],
            dst_ref=out_ref.at[0, me_time],
            send_sem=sends.at[distance],
            recv_sem=arrivals.at[distance],
            device_id=(target, me_chan),
            device_id_type=pl.DeviceIdType.MESH,
        )

    def source(distance):
        return lax.rem(me_time - distance + time_count, time_count)

    def arrival(distance):
        return pltpu.make_async_remote_copy(
            src_ref=white_ref.at[source(distance)],
            dst_ref=out_ref.at[0, source(distance)],
            send_sem=sends.at[distance],
            recv_sem=arrivals.at[distance],
            device_id=(source(distance), me_chan),
            device_id_type=pl.DeviceIdType.MESH,
        )

    def hop(piece, distance):
        return pltpu.make_async_remote_copy(
            src_ref=out_ref.at[piece - 1, source(distance)],
            dst_ref=out_ref.at[piece, source(distance)],
            send_sem=hops.at[piece, distance],
            recv_sem=landings.at[piece, distance],
            device_id=(me_time, below),
            device_id_type=pl.DeviceIdType.MESH,
        )

    for distance in range(1, time_count):
        regroup(distance).start()
    out_ref[0, me_time] = white_ref[me_time]

    for turn in range(time_count + piece_count - 1):
        for piece in range(piece_count):
            distance = turn - piece
            if not 0 <= distance < time_count:
                continue
            held = me_chan + piece < chan_count
            if piece == 0:
                if distance > 0:
                    arrival(distance).wait_recv()
            else:

                @pl.when(held)
                def _():
                    hop(piece, distance).wait_recv()

                @pl.when(~held)
                def _():
                    out_ref[piece, source(distance)] = jnp.zeros(
                        out_ref.shape[2:], out_ref.dtype
                    )

            if piece + 1 < piece_count:

                @pl.when(held & (me_chan > 0))
                def _():
                    hop(piece + 1, distance).start()

    for distance in range(1, time_count):
        regroup(distance).wait_send()
    for piece in range(1, piece_count):
        for distance in range(time_count):

            @pl.when((me_chan + piece - 1 < chan_count) & (me_chan > 0))
            def _():
                hop(piece, distance).wait_send()


def gather_pieces(whitened, piece_count):
    time_count = lax.axis_size("tm")
    chan_count = lax.axis_size("chan")
    return pl.pallas_call(
        functools.partial(gather_kernel, time_count, chan_count),
        in_specs=[pl.BlockSpec(memory_space=pltpu.VMEM)],
        out_specs=pl.BlockSpec(memory_space=pltpu.VMEM),
        out_shape=jax.ShapeDtypeStruct((piece_count,) + whitened.shape, jnp.bfloat16),
        scratch_shapes=[
            pltpu.SemaphoreType.DMA((time_count,)),
            pltpu.SemaphoreType.DMA((time_count,)),
            pltpu.SemaphoreType.DMA((piece_count, time_count)),
            pltpu.SemaphoreType.DMA((piece_count, time_count)),
        ],
        compiler_params=pltpu.CompilerParams(
            collective_id=0, has_side_effects=True, vmem_limit_bytes=24 * 2**20
        ),
        name="gather_pieces",
    )(whitened)


def gram_kernel(pieces_ref, out_ref):
    piece_count, time_count, _, width = pieces_ref.shape
    bins = out_ref.shape[1]
    band = out_ref.shape[3]
    rows = time_count * 2 * WPD
    window_count = rows // 2
    groups = [pieces_ref[piece].astype(jnp.float32) for piece in range(piece_count)]
    row = lax.broadcasted_iota(jnp.int32, (rows, rows), 0)
    column = lax.broadcasted_iota(jnp.int32, (rows, rows), 1)
    first_half = row % 8 < 4
    swap = jnp.where(
        first_half & (column == row + 4),
        1.0,
        jnp.where(~first_half & (column == row - 4), -1.0, 0.0),
    ).astype(jnp.bfloat16)
    lane = lax.broadcasted_iota(jnp.int32, (width, width), 0)
    mirror_lane = lax.broadcasted_iota(jnp.int32, (width, width), 1)
    mirror = jnp.where(lane + mirror_lane == width - 1, 1.0, 0.0).astype(jnp.bfloat16)
    upside_down = 7 - lax.broadcasted_iota(jnp.int32, (8, band), 0)
    contract = (((0,), (0,)), ((), ()))
    span = piece_count * width
    for f in range(bins):
        pieces = [
            group[:, f * 2 * WPD : (f + 1) * 2 * WPD].reshape(rows, width).astype(jnp.bfloat16)
            for group in groups
        ]
        own = jnp.dot(pieces[0], mirror, preferred_element_type=jnp.float32).astype(jnp.bfloat16)
        rotated = jnp.dot(swap, own, preferred_element_type=jnp.float32).astype(jnp.bfloat16)
        joined = jnp.concatenate(pieces, 1)
        if span < band + width:
            joined = jnp.concatenate(
                [joined, jnp.zeros((rows, band + width - span), jnp.bfloat16)], 1
            )
        for part, left in enumerate((own, rotated)):
            gram = lax.dot_general(left, joined, contract, preferred_element_type=jnp.float32)
            skewed = pltpu.roll(gram, band + 1, 1, stride=1, stride_axis=0)
            for first in range(0, width, 8):
                rows_of_eight = skewed[width - 8 - first : width - first, :band]
                out_ref[part, f, first : first + 8] = jnp.take_along_axis(
                    rows_of_eight, upside_down, axis=0
                ) * (1.0 / window_count)


def stacked_bands(pieces):
    piece_count, time_count, rows, width = pieces.shape
    bins = rows // (2 * WPD)
    block = 2
    return pl.pallas_call(
        gram_kernel,
        grid=(bins // block,),
        in_specs=[
            pl.BlockSpec(
                (piece_count, time_count, block * 2 * WPD, width), lambda i: (0, 0, i, 0)
            )
        ],
        out_specs=pl.BlockSpec((2, block, width, BAND), lambda i: (0, i, 0, 0)),
        out_shape=jax.ShapeDtypeStruct((2, bins, width, BAND), jnp.float32),
        compiler_params=pltpu.CompilerParams(vmem_limit_bytes=48 * 2**20),
        name="stacked_bands",
    )(pieces)


def local(record, window_starts, alive_mask):
    window_length = record.shape[0]
    local_width = record.shape[1]
    index_time = lax.axis_index("tm")
    offsets = window_starts - index_time * window_length
    earlier_offsets = passed_along(offsets, "tm", 1)
    all_windows = tuple(range(WPD))
    tails = transform(record, earlier_offsets, 1, all_windows)
    following = passed_along(tails, "tm", -1)
    spectra = transform(record, offsets, 0, all_windows) + following
    whitened = whiten(spectra, alive_mask)
    time_count = lax.axis_size("tm")
    blocks = whitened.reshape(time_count, KEEP // time_count * 2 * WPD, local_width)
    piece_count = min(BAND // local_width + 1, lax.axis_size("chan"))
    return stacked_bands(gather_pieces(blocks, piece_count))


def solution(mesh):
    return jax.shard_map(
        local,
        mesh=mesh,
        in_specs=(P("tm", "chan"), P("tm"), P("chan")),
        out_specs=P(None, "tm", "chan", None),
        check_vma=False,
    )
```

```python
import functools
import math

import jax
import jax.numpy as jnp
import numpy as np
from jax import lax
from jax.experimental import pallas as pl
from jax.experimental.pallas import tpu as pltpu
from jax.sharding import PartitionSpec as P

KEEP = 288
FLO = 61
HALF = 32
BAND = 512
WPD = 4


epsilon = 1e-06


def passed_along(block, axis, distance):
    devices = range(lax.axis_size(axis))
    route = [(i - distance, i) for i in devices if i - distance in devices]
    return lax.ppermute(block, axis, route)


def base_tables(window_length, block_length):
    step_angle = 2.0 * np.pi / window_length
    bin_numbers = FLO - HALF + np.arange(KEEP + 2 * HALF)
    times = np.arange(block_length)
    firsts = np.arange(0, window_length, block_length)
    base = step_angle * (bin_numbers[:, None] * times[None, :] % window_length)
    shift = step_angle * (bin_numbers[:, None] * firsts[None, :] % window_length)
    tapering = 0.5 - 0.5 * np.cos(step_angle * (firsts[:, None, None] + times[None, None, :]))
    values = (np.cos(base), np.sin(base), np.cos(shift), np.sin(shift), tapering)
    return [value.astype(np.float32) for value in values]


def dft_kernel(tail, windows, offsets_ref, *refs):
    cos_ref, sin_ref, shift_cos_ref, shift_sin_ref, taper_ref, record_ref, out_ref, padded = refs
    bin_count, block_length = cos_ref.shape
    window_length, width = record_ref.shape
    step = pl.program_id(0)
    chosen = lax.broadcasted_iota(jnp.int32, shift_cos_ref.shape, 1) == step
    shift_cos = jnp.sum(jnp.where(chosen, shift_cos_ref[...], 0.0), 1, keepdims=True)
    shift_sin = jnp.sum(jnp.where(chosen, shift_sin_ref[...], 0.0), 1, keepdims=True)

    @pl.when(step == 0)
    def _():
        out_ref[...] = jnp.zeros_like(out_ref)

        @pl.loop(0, window_length // block_length)
        def _(number):
            rows = pl.ds(pl.multiple_of(number * block_length, block_length), block_length)
            loud = pl.ds(
                pl.multiple_of(number * block_length + tail * window_length, block_length),
                block_length,
            )
            silent = pl.ds(
                pl.multiple_of(number * block_length + (1 - tail) * window_length, block_length),
                block_length,
            )
            padded[loud, :] = record_ref[rows, :].astype(jnp.float32)
            padded[silent, :] = jnp.zeros((block_length, width), jnp.float32)

    pieces = []
    for first in range(0, block_length, 256):
        span = slice(first, first + 256)
        base_cos = cos_ref[:, span]
        base_sin = sin_ref[:, span]
        tapering = taper_ref[0, :, span]
        cosine = tapering * (base_cos * shift_cos - base_sin * shift_sin)
        sine = -tapering * (base_sin * shift_cos + base_cos * shift_sin)
        pieces.append(jnp.concatenate([cosine, sine], 0).astype(jnp.bfloat16))
    lookup = jnp.concatenate(pieces, 1)
    for number in range(0, len(windows), 2):
        frames = []
        for window in windows[number : number + 2]:
            start = jnp.clip(offsets_ref[window], 0, window_length - 1)
            rows = pl.ds(start + step * block_length, block_length)
            frames.append(padded[rows, :].astype(jnp.bfloat16))
        out_ref[:, number * width : (number + 2) * width] += jnp.dot(
            lookup, jnp.concatenate(frames, 1), preferred_element_type=jnp.float32
        )


def transform(record, offsets, tail, windows):
    window_length, width = record.shape
    count = len(windows)
    block_length = math.gcd(window_length, 1024)
    bin_count = KEEP + 2 * HALF
    steps = window_length // block_length
    return pl.pallas_call(
        functools.partial(dft_kernel, tail, windows),
        grid=(steps,),
        in_specs=[
            pl.BlockSpec(memory_space=pltpu.SMEM),
            pl.BlockSpec((bin_count, block_length), lambda i: (0, 0)),
            pl.BlockSpec((bin_count, block_length), lambda i: (0, 0)),
            pl.BlockSpec((bin_count, steps), lambda i: (0, 0)),
            pl.BlockSpec((bin_count, steps), lambda i: (0, 0)),
            pl.BlockSpec((1, 1, block_length), lambda i: (i, 0, 0)),
            pl.BlockSpec((window_length, width), lambda i: (0, 0)),
        ],
        out_specs=pl.BlockSpec((2 * bin_count, count * width), lambda i: (0, 0)),
        out_shape=jax.ShapeDtypeStruct((2 * bin_count, count * width), jnp.float32),
        scratch_shapes=[pltpu.VMEM((2 * window_length, width), jnp.float32)],
        compiler_params=pltpu.CompilerParams(vmem_limit_bytes=44 * 2**20),
        cost_estimate=pl.CostEstimate(
            flops=4 * bin_count * count * width * window_length,
            bytes_accessed=2 * width * window_length,
            transcendentals=0,
        ),
        name="windowed_transform",
    )(offsets, *base_tables(window_length, block_length), record)


def smoother_matrix():
    row_index = lax.iota(jnp.int32, KEEP)[:, None]
    column_index = lax.iota(jnp.int32, KEEP + 2 * HALF)[None, :]
    inside = (column_index >= row_index) & (column_index <= row_index + 2 * HALF)
    return inside.astype(jnp.float32)


def whiten(spectra, alive_mask):
    bin_count = KEEP + 2 * HALF
    width = alive_mask.shape[0]
    real_part = spectra[:bin_count]
    imag_part = spectra[bin_count:]
    magnitude = jnp.sqrt(real_part * real_part + imag_part * imag_part)
    smoothed = jnp.dot(smoother_matrix(), magnitude, precision=lax.Precision.HIGHEST)
    smoothed = smoothed / (2 * HALF + 1)
    scaling = jnp.tile(alive_mask.astype(jnp.float32), WPD)[None, :] / (smoothed + epsilon)
    white_real = real_part[HALF : HALF + KEEP] * scaling
    white_imag = imag_part[HALF : HALF + KEEP] * scaling
    whitened = jnp.concatenate([white_real, white_imag], 1).astype(jnp.bfloat16)
    return whitened.reshape(KEEP, 2 * WPD, width)


def gather_kernel(time_count, chan_count, white_ref, out_ref, sends, arrivals, hops, landings):
    piece_count = out_ref.shape[0]
    me_time = lax.axis_index("tm")
    me_chan = lax.axis_index("chan")
    below = lax.rem(me_chan + chan_count - 1, chan_count)
    above = lax.rem(me_chan + 1, chan_count)

    def signal(time, chan):
        pl.semaphore_signal(
            barrier, inc=1, device_id=(time, chan), device_id_type=pl.DeviceIdType.MESH
        )

    barrier = pltpu.get_barrier_semaphore()
    for distance in range(1, time_count):
        signal(lax.rem(me_time + distance, time_count), me_chan)
    signal(me_time, below)
    signal(me_time, above)
    pl.semaphore_wait(barrier, time_count + 1)

    def regroup(distance):
        target = lax.rem(me_time + distance, time_count)
        return pltpu.make_async_remote_copy(
            src_ref=white_ref.at[target],
            dst_ref=out_ref.at[0, me_time],
            send_sem=sends.at[distance],
            recv_sem=arrivals.at[distance],
            device_id=(target, me_chan),
            device_id_type=pl.DeviceIdType.MESH,
        )

    def source(distance):
        return lax.rem(me_time - distance + time_count, time_count)

    def arrival(distance):
        return pltpu.make_async_remote_copy(
            src_ref=white_ref.at[source(distance)],
            dst_ref=out_ref.at[0, source(distance)],
            send_sem=sends.at[distance],
            recv_sem=arrivals.at[distance],
            device_id=(source(distance), me_chan),
            device_id_type=pl.DeviceIdType.MESH,
        )

    def hop(piece, distance):
        return pltpu.make_async_remote_copy(
            src_ref=out_ref.at[piece - 1, source(distance)],
            dst_ref=out_ref.at[piece, source(distance)],
            send_sem=hops.at[piece, distance],
            recv_sem=landings.at[piece, distance],
            device_id=(me_time, below),
            device_id_type=pl.DeviceIdType.MESH,
        )

    for distance in range(1, time_count):
        regroup(distance).start()
    out_ref[0, me_time] = white_ref[me_time]

    for turn in range(time_count + piece_count - 1):
        for piece in range(piece_count):
            distance = turn - piece
            if not 0 <= distance < time_count:
                continue
            held = me_chan + piece < chan_count
            if piece == 0:
                if distance > 0:
                    arrival(distance).wait_recv()
            else:

                @pl.when(held)
                def _():
                    hop(piece, distance).wait_recv()

                @pl.when(~held)
                def _():
                    out_ref[piece, source(distance)] = jnp.zeros(
                        out_ref.shape[2:], out_ref.dtype
                    )

            if piece + 1 < piece_count:

                @pl.when(held & (me_chan > 0))
                def _():
                    hop(piece + 1, distance).start()

    for distance in range(1, time_count):
        regroup(distance).wait_send()
    for piece in range(1, piece_count):
        for distance in range(time_count):

            @pl.when((me_chan + piece - 1 < chan_count) & (me_chan > 0))
            def _():
                hop(piece, distance).wait_send()


def gather_pieces(whitened, piece_count):
    time_count = lax.axis_size("tm")
    chan_count = lax.axis_size("chan")
    return pl.pallas_call(
        functools.partial(gather_kernel, time_count, chan_count),
        in_specs=[pl.BlockSpec(memory_space=pltpu.VMEM)],
        out_specs=pl.BlockSpec(memory_space=pltpu.VMEM),
        out_shape=jax.ShapeDtypeStruct((piece_count,) + whitened.shape, jnp.bfloat16),
        scratch_shapes=[
            pltpu.SemaphoreType.DMA((time_count,)),
            pltpu.SemaphoreType.DMA((time_count,)),
            pltpu.SemaphoreType.DMA((piece_count, time_count)),
            pltpu.SemaphoreType.DMA((piece_count, time_count)),
        ],
        compiler_params=pltpu.CompilerParams(
            collective_id=0, has_side_effects=True, vmem_limit_bytes=24 * 2**20
        ),
        name="gather_pieces",
    )(whitened)


def gram_kernel(pieces_ref, out_ref):
    piece_count, time_count, _, width = pieces_ref.shape
    bins = out_ref.shape[1]
    band = out_ref.shape[3]
    rows = time_count * 2 * WPD
    window_count = rows // 2
    groups = [pieces_ref[piece].astype(jnp.float32) for piece in range(piece_count)]
    row = lax.broadcasted_iota(jnp.int32, (rows, rows), 0)
    column = lax.broadcasted_iota(jnp.int32, (rows, rows), 1)
    first_half = row % 8 < 4
    swap = jnp.where(
        first_half & (column == row + 4),
        1.0,
        jnp.where(~first_half & (column == row - 4), -1.0, 0.0),
    ).astype(jnp.bfloat16)
    lane = lax.broadcasted_iota(jnp.int32, (width, width), 0)
    mirror_lane = lax.broadcasted_iota(jnp.int32, (width, width), 1)
    mirror = jnp.where(lane + mirror_lane == width - 1, 1.0, 0.0).astype(jnp.bfloat16)
    upside_down = 7 - lax.broadcasted_iota(jnp.int32, (8, band), 0)
    contract = (((0,), (0,)), ((), ()))
    span = piece_count * width
    for f in range(bins):
        pieces = [
            group[:, f * 2 * WPD : (f + 1) * 2 * WPD].reshape(rows, width).astype(jnp.bfloat16)
            for group in groups
        ]
        own = jnp.dot(pieces[0], mirror, preferred_element_type=jnp.float32).astype(jnp.bfloat16)
        rotated = jnp.dot(swap, own, preferred_element_type=jnp.float32).astype(jnp.bfloat16)
        joined = jnp.concatenate(pieces, 1)
        if span < band + width:
            joined = jnp.concatenate(
                [joined, jnp.zeros((rows, band + width - span), jnp.bfloat16)], 1
            )
        for part, left in enumerate((own, rotated)):
            gram = lax.dot_general(left, joined, contract, preferred_element_type=jnp.float32)
            skewed = pltpu.roll(gram, band + 1, 1, stride=1, stride_axis=0)
            for first in range(0, width, 8):
                rows_of_eight = skewed[width - 8 - first : width - first, :band]
                out_ref[part, f, first : first + 8] = jnp.take_along_axis(
                    rows_of_eight, upside_down, axis=0
                ) * (1.0 / window_count)


def stacked_bands(pieces):
    piece_count, time_count, rows, width = pieces.shape
    bins = rows // (2 * WPD)
    block = 2
    return pl.pallas_call(
        gram_kernel,
        grid=(bins // block,),
        in_specs=[
            pl.BlockSpec(
                (piece_count, time_count, block * 2 * WPD, width), lambda i: (0, 0, i, 0)
            )
        ],
        out_specs=pl.BlockSpec((2, block, width, BAND), lambda i: (0, i, 0, 0)),
        out_shape=jax.ShapeDtypeStruct((2, bins, width, BAND), jnp.float32),
        compiler_params=pltpu.CompilerParams(vmem_limit_bytes=48 * 2**20),
        name="stacked_bands",
    )(pieces)


def local(record, window_starts, alive_mask):
    window_length = record.shape[0]
    local_width = record.shape[1]
    index_time = lax.axis_index("tm")
    offsets = window_starts - index_time * window_length
    earlier_offsets = passed_along(offsets, "tm", 1)
    all_windows = tuple(range(WPD))
    tails = transform(record, earlier_offsets, 1, all_windows)
    following = passed_along(tails, "tm", -1)
    spectra = transform(record, offsets, 0, all_windows) + following
    whitened = whiten(spectra, alive_mask)
    time_count = lax.axis_size("tm")
    blocks = whitened.reshape(time_count, KEEP // time_count * 2 * WPD, local_width)
    piece_count = min(BAND // local_width + 1, lax.axis_size("chan"))
    return stacked_bands(gather_pieces(blocks, piece_count))


def solution(mesh):
    return jax.shard_map(
        local,
        mesh=mesh,
        in_specs=(P("tm", "chan"), P("tm"), P("chan")),
        out_specs=P(None, "tm", "chan", None),
        check_vma=False,
    )
```
